32 devices in a mesh: row: 2 (over core), lat: 8 (over z, x), grp: 2 (over y).
Axes of the slice: x: 2, y: 2, z: 4, core: 2. Of those that a mesh axis runs over, the one named last changes fastest.
Arguments:
- stream_in: bfloat16 [192, 3584], P(('lat', 'grp'), 'row'), may hold values from -36 to 36, as said below
- pre_gain: float32 [3584], P('row'), may hold values from 0.25 to 1.75
- gate_weight: bfloat16 [3584, 14336], P('row', ('lat', 'grp')), may hold values from -0.09375 to 0.09375
- up_weight: bfloat16 [3584, 14336], P('row', ('lat', 'grp')), may hold values from -0.09375 to 0.09375
- down_weight: bfloat16 [14336, 3584], P(('lat', 'grp'), 'row'), may hold values from -0.046875 to 0.046875
- post_gain: float32 [3584], P('row'), may hold values from 0.25 to 1.75
- enc_weight: float32 [3584, 16384], P('row', ('lat', 'grp')), may hold values from -0.09375 to 0.09375
- enc_bias: float32 [16384], P(('lat', 'grp')), may hold values from -3 to 3
- dec_weight: float32 [16384, 3584], P(('lat', 'grp'), 'row'), may hold values from -0.046875 to 0.046875
- dec_bias: float32 [3584], P('row'), may hold values from -3 to 3
Outputs:
- stream_out: bfloat16 [192, 3584], P(('lat', 'grp'), 'row')
- grad_enc: float32 [3584, 16384], P('row', ('lat', 'grp'))
- grad_enc_bias: float32 [16384], P(('lat', 'grp'))
- grad_dec: float32 [16384, 3584], P(('lat', 'grp'), 'row')
- grad_dec_bias: float32 [3584], P('row')
The draws below stay inside these ranges and needn't reach their ends.
Inputs may be any that keep to these rules, and one draw needn't show every extreme that they name: `stream_in`: Real-valued activations with scales that differ over rows and features.
All inputs are finite; a program needn't handle non-finite values.
Results may differ from the reference program's by a relative error of at most 0.013.
Values may be sent and summed in bfloat16 or wider, within the bound.
A program may use at most 128 MiB of HBM per device.

```python
import math
import jax
import jax.numpy as jnp
from jax import lax

D = 3584
FF = 14336
LATENTS = 16384
TOKENS = 192


def draw_stream_in(key, part):
    keys = jax.random.split(jax.random.fold_in(key, 11), 3)
    row_scale = jnp.exp(jax.random.uniform(keys[0], (TOKENS, 1), jnp.float32, math.log(0.3), math.log(3.0)))
    col_scale = jnp.exp(jax.random.uniform(keys[1], (1, D), jnp.float32, math.log(0.3), math.log(3.0)))
    base = jnp.clip(jax.random.normal(keys[2], (TOKENS, D), jnp.float32), -4.0, 4.0)
    return (base * row_scale * col_scale).astype(jnp.bfloat16)


def shard_levels(own_key, dims, shards, low, high):
    gain = 1.0
    for position, parts in shards:
        draws = jax.random.uniform(jax.random.fold_in(jax.random.fold_in(own_key, 6), position), (parts,), jnp.float32, low / len(shards), high / len(shards))
        gain = gain * jnp.repeat(jnp.exp(draws), dims[position] // parts).reshape((-1,) + (1,) * (len(dims) - 1 - position))
    return gain


def normal_values(own_key, dims, width, most, shards=(), kind=jnp.bfloat16):
    values = width * jax.random.normal(own_key, dims, jnp.float32)
    if shards:
        values = values * shard_levels(own_key, dims, shards, -0.22, 0.18)
    return jnp.clip(values, -most, most).astype(kind)


def setup_inputs(seed: int = 0) -> dict:
    key_of = jax.random.split(jax.random.key(seed), 11)
    stream_in = draw_stream_in(jax.random.fold_in(key_of[10], 71), 0)
    pre_gain = jnp.clip(1.0 + 0.15 * jax.random.normal(key_of[1], (D,), jnp.float32), 0.25, 1.75)
    gate_weight = normal_values(key_of[2], (D, FF), D ** -0.5, 0.09375, ((0, 2), (1, 16)))
    up_weight = normal_values(key_of[3], (D, FF), D ** -0.5, 0.09375, ((0, 2), (1, 16)))
    down_weight = normal_values(key_of[4], (FF, D), FF ** -0.5, 0.046875, ((0, 16), (1, 2)))
    post_gain = jnp.clip(1.0 + 0.15 * jax.random.normal(key_of[5], (D,), jnp.float32), 0.25, 1.75)
    enc_weight = normal_values(key_of[6], (D, LATENTS), D ** -0.5, 0.09375, ((0, 2), (1, 16)), jnp.float32)
    enc_bias = normal_values(key_of[7], (LATENTS,), 0.5, 3.0, ((0, 16),), jnp.float32)
    dec_weight = normal_values(key_of[8], (LATENTS, D), LATENTS ** -0.5, 0.046875, ((0, 16), (1, 2)), jnp.float32)
    dec_bias = normal_values(key_of[9], (D,), 0.5, 3.0, ((0, 2),), jnp.float32)
    return {"stream_in": stream_in, "pre_gain": pre_gain, "gate_weight": gate_weight, "up_weight": up_weight, "down_weight": down_weight, "post_gain": post_gain, "enc_weight": enc_weight, "enc_bias": enc_bias, "dec_weight": dec_weight, "dec_bias": dec_bias}


epsilon = 1e-06
sparsity = 0.2
sharpness = 4.0

def reference(stream_in, pre_gain, gate_weight, up_weight, down_weight, post_gain, enc_weight, enc_bias, dec_weight, dec_bias):
    highest = lax.Precision.HIGHEST
    stream = stream_in.astype(jnp.float32)
    squares = lax.optimization_barrier(jnp.mean(stream * stream, axis=1, keepdims=True))
    normed = (stream * lax.rsqrt(squares + epsilon) * pre_gain).astype(jnp.bfloat16)
    gate = jnp.dot(normed, gate_weight, preferred_element_type=jnp.float32)
    upward = jnp.dot(normed, up_weight, preferred_element_type=jnp.float32)
    hidden = (jax.nn.gelu(gate, approximate=True) * upward).astype(jnp.bfloat16)
    output = jnp.dot(hidden, down_weight, preferred_element_type=jnp.float32)
    out_squares = lax.optimization_barrier(jnp.mean(output * output, axis=1, keepdims=True))
    stream_out = (stream + output * lax.rsqrt(out_squares + epsilon) * post_gain).astype(jnp.bfloat16)
    inputs = stream_out.astype(jnp.float32)
    scale = 1.0 / jnp.sqrt(jnp.float32(TOKENS))
    preact = jnp.dot(inputs, enc_weight, precision=highest, preferred_element_type=jnp.float32) + enc_bias
    latents = jax.nn.softplus(sharpness * preact) / sharpness
    recon = jnp.dot(latents, dec_weight, precision=highest, preferred_element_type=jnp.float32) + dec_bias
    residual_grad = (recon - inputs) * scale
    grad_dec = jnp.dot(latents.T, residual_grad, precision=highest, preferred_element_type=jnp.float32)
    grad_dec_bias = lax.optimization_barrier(jnp.sum(residual_grad, axis=0))
    latent_grad = jnp.dot(residual_grad, dec_weight.T, precision=highest, preferred_element_type=jnp.float32) + sparsity * scale
    preact_grad = latent_grad * jax.nn.sigmoid(sharpness * preact)
    grad_enc = jnp.dot(inputs.T, preact_grad, precision=highest, preferred_element_type=jnp.float32)
    grad_enc_bias = lax.optimization_barrier(jnp.sum(preact_grad, axis=0))
    return (stream_out, grad_enc, grad_enc_bias, grad_dec, grad_dec_bias)
```

```python
import functools
import math

import jax
import jax.numpy as jnp
from jax import lax
from jax.experimental import pallas as pl
from jax.experimental.pallas import tpu as pltpu
from jax.sharding import PartitionSpec as P

epsilon = 1e-06
sparsity = 0.2
sharpness = 4.0
PAD = 16
f32 = jnp.float32
bf16 = jnp.bfloat16
MESH = pl.DeviceIdType.MESH


def each(n, f):
    if n > 0:
        lax.fori_loop(0, n, lambda i, c: (f(i), c)[1], 0)


def column_tiles(width, f, tile=256):
    whole = width // tile
    each(whole, lambda i: f(pl.ds(pl.multiple_of(i * tile, tile), tile)))
    if width % tile:
        f(pl.ds(whole * tile, width % tile))


def kernel(
    shape,
    stream_ref, pre_ref, post_ref, encb_ref, decb_ref,
    gate_hbm, up_hbm, down_hbm, enc_hbm, dec_hbm,
    out_ref, inputs_ref, lat_ref, resid_ref, pgrad_ref, gencb_ref, gdecb_ref,
    wg, wu, wd, wenc, wdec, enc16, dec16,
    xs, xg, gbuf, ubuf, sbuf, hidden, squares,
    part1, land1, mid1, far1, tbuf, ys,
    pbuf, preact, part2, land2, mid2, far2, rs, bbuf,
    wsem,
    ag_send, ag_recv, rs_send, rs_recv, rz_send, rz_recv, row_send, row_recv,
):
    rows, zs, qs, grps, real, width, tokens = shape
    n = zs * qs
    total = n * PAD
    row = lax.axis_index("row")
    me = lax.axis_index("lat") * grps + lax.axis_index("grp")
    z = me // qs
    q = lax.rem(me, qs)

    def at(shard):
        return {"lat": shard // grps, "grp": lax.rem(shard, grps)}

    def zpeer(d):
        return lax.rem(z + d, zs)

    def qpeer(d):
        return lax.rem(q + d, qs)

    def send(src, dst, s, r, dev):
        return pltpu.make_async_remote_copy(
            src_ref=src, dst_ref=dst, send_sem=s, recv_sem=r, device_id=dev, device_id_type=MESH
        )

    loads = [
        pltpu.make_async_copy(a, b, wsem.at[i])
        for i, (a, b) in enumerate(
            [(gate_hbm, wg), (up_hbm, wu), (down_hbm, wd), (enc_hbm, wenc), (dec_hbm, wdec)]
        )
    ]
    for load in loads:
        load.start()

    barrier = pltpu.get_barrier_semaphore()

    def hail(dev):
        pl.semaphore_signal(barrier, inc=1, device_id=dev, device_id_type=MESH)

    each(zs - 1, lambda i: hail(at(zpeer(i + 1) * qs + q)))
    each(qs - 1, lambda i: hail(at(z * qs + qpeer(i + 1))))
    each(rows - 1, lambda i: hail({"row": lax.rem(row + i + 1, rows)}))
    pl.semaphore_wait(barrier, zs - 1 + qs - 1 + rows - 1)

    def gather_copy(k, buf, shard, dev, slot):
        return send(buf.at[shard], buf.at[shard], ag_send.at[k, slot], ag_recv.at[k, shard], dev)

    def to_plane(k, buf, dz, shard, start):
        def one(i):
            c = gather_copy(k, buf, shard, at(z * qs + qpeer(i + 1)), dz * qs + i + 1)
            c.start() if start else c.wait_send()

        each(qs - 1, one)

    def gather_start(k, buf):
        each(
            zs - 1,
            lambda i: gather_copy(k, buf, me, at(zpeer(i + 1) * qs + q), (i + 1) * qs).start(),
        )
        to_plane(k, buf, 0, me, True)

    def gather_pass(k, buf):
        def one(i):
            shard = zpeer(i + 1) * qs + q
            gather_copy(k, buf, shard, at(shard), 0).wait_recv()
            to_plane(k, buf, i + 1, shard, True)

        each(zs - 1, one)

    def gather_end(k, buf):
        def one(dz):
            def two(i):
                shard = zpeer(dz) * qs + qpeer(i + 1)
                gather_copy(k, buf, shard, at(z * qs + qpeer(i + 1)), 0).wait_recv()

            each(qs - 1, two)

        each(zs, one)

        def sent(dz):
            to_plane(k, buf, dz, zpeer(dz) * qs + q, False)

        each(zs, sent)
        each(
            zs - 1,
            lambda i: gather_copy(k, buf, me, at(zpeer(i + 1) * qs + q), (i + 1) * qs).wait_send(),
        )

    def plane_out(k, part, land, zz, dq):
        to = qpeer(dq)
        return send(
            part.at[zz * qs + to], land.at[q, zz],
            rs_send.at[k, zz * qs + dq], rs_recv.at[k, zz * qs + q], at(z * qs + to),
        )

    def plane_in(k, part, land, zz, dq):
        of = qpeer(dq)
        return send(
            part.at[zz * qs + of], land.at[of, zz],
            rs_send.at[k, zz * qs + dq], rs_recv.at[k, zz * qs + of], at(z * qs + of),
        )

    def line(k, mid, far, dz):
        to = zpeer(dz)
        return send(mid.at[to], far.at[z], rz_send.at[k, to], rz_recv.at[k, z], at(to * qs + q))

    def line_in(k, mid, far, dz):
        of = zpeer(dz)
        return send(mid.at[of], far.at[of], rz_send.at[k, of], rz_recv.at[k, of], at(of * qs + q))

    def scatter_start(k, part, land):
        def one(dz):
            zz = zpeer(dz + 1)
            each(qs - 1, lambda i: plane_out(k, part, land, zz, i + 1).start())

        each(zs, one)

    def scatter_sum(k, part, land, mid, far):
        def plane_sum(zz):
            each(qs - 1, lambda i: plane_in(k, part, land, zz, i + 1).wait_recv())
            acc = part[zz * qs + q].astype(f32)
            for i in range(1, qs):
                acc = acc + land[qpeer(i), zz].astype(f32)
            return acc

        def one(i):
            zz = zpeer(i + 1)
            mid[zz] = plane_sum(zz).astype(bf16)
            line(k, mid, far, i + 1).start()

        each(zs - 1, one)
        acc = plane_sum(z)
        for dz in range(1, zs):
            line_in(k, mid, far, dz).wait_recv()
            acc = acc + far[zpeer(dz)].astype(f32)
        return acc

    def scatter_end(k, part, land, mid, far):
        def one(dz):
            each(qs - 1, lambda i: plane_out(k, part, land, zpeer(dz), i + 1).wait_send())

        each(zs, one)
        each(zs - 1, lambda i: line(k, mid, far, i + 1).wait_send())

    def row_out(k, buf, d):
        return send(
            buf.at[row], buf.at[row], row_send.at[k, d], row_recv.at[k, row],
            {"row": lax.rem(row + d, rows)},
        )

    def row_start(k, buf):
        each(rows - 1, lambda i: row_out(k, buf, i + 1).start())

    def row_wait(k, buf):
        def one(i):
            of = lax.rem(row + i + 1, rows)
            send(
                buf.at[of], buf.at[of], row_send.at[k, 0], row_recv.at[k, of], {"row": of}
            ).wait_recv()
            row_out(k, buf, i + 1).wait_send()

        each(rows - 1, one)

    def row_sum(buf, *index):
        acc = buf[(0, *index)].astype(f32)
        for i in range(1, rows):
            acc = acc + buf[(i, *index)].astype(f32)
        return acc

    def block(i):
        return pl.ds(pl.multiple_of(i * PAD, PAD), PAD)

    def cast(src, dst):
        tall = src.shape[0]
        chunk = 16

        def one(i):
            r = pl.ds(pl.multiple_of(i * chunk, chunk), chunk)
            dst[r, :] = src[r, :].astype(bf16)

        each(tall // chunk, one)

    xs[me] = stream_ref[...]
    gather_start(0, xs)
    gather_pass(0, xs)
    gather_end(0, xs)

    def norm_rows(i):
        x = xs[i].astype(f32)
        xg[block(i), :] = (x * pre_ref[...]).astype(bf16)
        sbuf[row, block(i), :] = jnp.broadcast_to(
            jnp.sum(x * x, axis=1, keepdims=True), (PAD, 128)
        )

    each(n, norm_rows)
    row_start(0, sbuf)

    def project(buf, w):
        def one(c):
            buf[row, :, c] = jnp.dot(xg[...], w[:, c], preferred_element_type=f32).astype(bf16)

        column_tiles(w.shape[1], one)

    loads[0].wait()
    project(gbuf, wg)
    row_start(1, gbuf)
    loads[1].wait()
    project(ubuf, wu)
    row_start(2, ubuf)
    loads[3].wait()
    row_wait(0, sbuf)
    row_wait(1, gbuf)
    row_wait(2, ubuf)

    def activate(i):
        r = lax.rsqrt(row_sum(sbuf, block(i))[:, :1] / width + epsilon)
        g = row_sum(gbuf, block(i)) * r
        u = row_sum(ubuf, block(i)) * r
        hidden[block(i), :] = (jax.nn.gelu(g, approximate=True) * u).astype(bf16)

    each(n, activate)
    loads[2].wait()

    def down(c):
        v = jnp.dot(hidden[...], wd[:, c], preferred_element_type=f32)
        part1[:, :, c] = v.astype(bf16).reshape(n, PAD, v.shape[1])

    column_tiles(wd.shape[1], down)
    scatter_start(0, part1, land1)
    cast(wenc, enc16)
    output = scatter_sum(0, part1, land1, mid1, far1)
    tbuf[row] = jnp.broadcast_to(jnp.sum(output * output, axis=1, keepdims=True), (PAD, 128))
    row_start(3, tbuf)
    row_wait(3, tbuf)
    scale_out = lax.rsqrt(row_sum(tbuf)[:, :1] / width + epsilon)
    mine = stream_ref[...].astype(f32) + output * scale_out * post_ref[...]
    stream_out = mine.astype(bf16)
    out_ref[...] = stream_out
    ys[me] = stream_out
    gather_start(1, ys)
    scatter_end(0, part1, land1, mid1, far1)
    loads[4].wait()
    gather_pass(1, ys)
    cast(wdec, dec16)
    gather_end(1, ys)
    inputs_ref[...] = ys[...].reshape(total, ys.shape[2])

    def encode(c):
        pbuf[row, :, c] = jnp.dot(
            ys[...].reshape(total, ys.shape[2]), enc16[:, c], preferred_element_type=f32
        ).astype(bf16)

    column_tiles(enc16.shape[1], encode)
    row_start(4, pbuf)
    row_wait(4, pbuf)

    def softplus(i):
        p = sharpness * (row_sum(pbuf, block(i)) + encb_ref[...])
        e = jnp.exp(-jnp.abs(p))
        lat_ref[block(i), :] = (
            (jnp.maximum(p, 0.0) + jnp.log1p(e)) * (1.0 / sharpness)
        ).astype(bf16)
        preact[block(i), :] = jnp.where(p >= 0, 1.0, e) / (1.0 + e)

    each(n, softplus)

    def decode(c):
        v = jnp.dot(lat_ref[...], dec16[:, c], preferred_element_type=f32)
        part2[:, :, c] = v.astype(bf16).reshape(n, PAD, v.shape[1])

    column_tiles(dec16.shape[1], decode)
    scatter_start(1, part2, land2)
    recon = scatter_sum(1, part2, land2, mid2, far2)
    scale = 1.0 / math.sqrt(tokens)
    keep = lax.broadcasted_iota(jnp.int32, (PAD, 1), 0) < real
    resid = jnp.where(keep, (recon + decb_ref[...] - ys[me].astype(f32)) * scale, 0.0)
    rs[me] = resid.astype(bf16)
    gather_start(2, rs)
    scatter_end(1, part2, land2, mid2, far2)
    gather_pass(2, rs)
    gather_end(2, rs)
    resid_ref[...] = rs[...].reshape(total, rs.shape[2])

    def back(c):
        bbuf[row, :, c] = lax.dot_general(
            rs[...].reshape(total, rs.shape[2]), dec16[c, :],
            (((1,), (1,)), ((), ())), preferred_element_type=f32,
        ).astype(bf16)

    column_tiles(dec16.shape[0], back)
    row_start(5, bbuf)

    gdecb_ref[...] = jnp.zeros_like(gdecb_ref)

    def dec_bias(i):
        gdecb_ref[...] += jnp.sum(rs[i].astype(f32), axis=0, keepdims=True)

    each(n, dec_bias)
    row_wait(5, bbuf)
    gencb_ref[...] = jnp.zeros_like(gencb_ref)

    def finish(i):
        g = (row_sum(bbuf, block(i)) + sparsity * scale) * preact[block(i), :]
        pgrad_ref[block(i), :] = g.astype(bf16)
        gencb_ref[...] += jnp.sum(jnp.where(keep, g, 0.0), axis=0, keepdims=True)

    each(n, finish)


def body(
    split, sizes,
    stream_in, pre_gain, gate_weight, up_weight, down_weight, post_gain,
    enc_weight, enc_bias, dec_weight, dec_bias,
):
    rows, zs, qs, grps = sizes
    n = zs * qs
    real, d = stream_in.shape
    hid = gate_weight.shape[1]
    lat = enc_weight.shape[1]
    total = n * PAD
    shape = (rows, zs, qs, grps, real, d * rows, real * n)
    vmem = pltpu.VMEM
    scratch = [
        vmem((d, hid), bf16), vmem((d, hid), bf16), vmem((hid, d), bf16),
        vmem((d, lat), f32), vmem((lat, d), f32), vmem((d, lat), bf16), vmem((lat, d), bf16),
        vmem((n, PAD, d), bf16), vmem((total, d), bf16),
        vmem((rows, total, hid), bf16), vmem((rows, total, hid), bf16),
        vmem((rows, total, 128), f32), vmem((total, hid), bf16), vmem((8, 128), f32),
        vmem((n, PAD, d), bf16), vmem((qs, zs, PAD, d), bf16),
        vmem((zs, PAD, d), bf16), vmem((zs, PAD, d), bf16),
        vmem((rows, PAD, 128), f32), vmem((n, PAD, d), bf16),
        vmem((rows, total, lat), bf16), vmem((total, lat), f32),
        vmem((n, PAD, d), bf16), vmem((qs, zs, PAD, d), bf16),
        vmem((zs, PAD, d), bf16), vmem((zs, PAD, d), bf16),
        vmem((n, PAD, d), bf16), vmem((rows, total, lat), bf16),
        pltpu.SemaphoreType.DMA((5,)),
        pltpu.SemaphoreType.DMA((3, n)), pltpu.SemaphoreType.DMA((3, n)),
        pltpu.SemaphoreType.DMA((2, n)), pltpu.SemaphoreType.DMA((2, n)),
        pltpu.SemaphoreType.DMA((2, zs)), pltpu.SemaphoreType.DMA((2, zs)),
        pltpu.SemaphoreType.DMA((6, rows)), pltpu.SemaphoreType.DMA((6, rows)),
    ]
    here = pl.BlockSpec(memory_space=pltpu.VMEM)
    there = pl.BlockSpec(memory_space=pl.ANY)
    sds = jax.ShapeDtypeStruct
    padded = jnp.pad(stream_in, ((0, PAD - real), (0, 0)))
    out, inputs, latents, resid, pgrad, gencb, gdecb = pl.pallas_call(
        functools.partial(kernel, shape),
        out_shape=(
            sds((PAD, d), bf16), sds((total, d), bf16), sds((total, lat), bf16),
            sds((total, d), bf16), sds((total, lat), bf16), sds((1, lat), f32), sds((1, d), f32),
        ),
        in_specs=[here] * 5 + [there] * 5,
        out_specs=[here] * 7,
        scratch_shapes=scratch,
        compiler_params=pltpu.CompilerParams(
            collective_id=0, has_side_effects=True, vmem_limit_bytes=60 * 1024 * 1024
        ),
    )(
        padded, pre_gain[None], post_gain[None], enc_bias[None], dec_bias[None],
        gate_weight, up_weight, down_weight, enc_weight, dec_weight,
    )
    grad_dec = jnp.dot(latents.T, resid, preferred_element_type=f32)
    grad_enc = jnp.dot(inputs.T, pgrad, preferred_element_type=f32)
    return (out[:real], grad_enc, gencb[0], grad_dec, gdecb[0])


def solution(mesh):
    rows, lats, grps = (mesh.shape[a] for a in ("row", "lat", "grp"))
    inner = max(i for i in range(1, lats + 1) if lats % i == 0 and i * i <= lats)
    sizes = (rows, lats // inner, inner * grps, grps)
    both = ("lat", "grp")
    placed = (
        P(both, "row"), P("row"), P("row", both), P("row", both), P(both, "row"),
        P("row"), P("row", both), P(both), P(both, "row"), P("row"),
    )
    return jax.shard_map(
        functools.partial(body, None, sizes),
        mesh=mesh,
        in_specs=placed,
        out_specs=(P(both, "row"), P("row", both), P(both), P(both, "row"), P("row")),
        check_vma=False,
    )
```

```python
import functools
import math

import jax
import jax.numpy as jnp
from jax import lax
from jax.experimental import pallas as pl
from jax.experimental.pallas import tpu as pltpu
from jax.sharding import PartitionSpec as P

epsilon = 1e-06
sparsity = 0.2
sharpness = 4.0
PAD = 16
f32 = jnp.float32
bf16 = jnp.bfloat16
MESH = pl.DeviceIdType.MESH


def each(n, f):
    if n > 0:
        lax.fori_loop(0, n, lambda i, c: (f(i), c)[1], 0)


def column_tiles(width, f, tile=256):
    whole = width // tile
    each(whole, lambda i: f(pl.ds(pl.multiple_of(i * tile, tile), tile)))
    if width % tile:
        f(pl.ds(whole * tile, width % tile))


def kernel(
    shape,
    stream_hbm, pre_hbm, post_hbm, encb_hbm, decb_hbm,
    gate_hbm, up_hbm, down_hbm, enc_hbm, dec_hbm,
    out_ref, inputs_ref, lat_ref, resid_ref, pgrad_ref, gencb_ref, gdecb_ref,
    wg, wu, wd, wenc, wdec, enc16, dec16,
    xs, xg, gbuf, ubuf, sbuf, hidden, squares,
    part1, land1, mid1, far1, tbuf, ys,
    pbuf, preact, part2, land2, mid2, far2, rs, bbuf,
    pre_ref, post_ref, encb_ref, decb_ref,
    wsem,
    ag_send, ag_recv, rs_send, rs_recv, rz_send, rz_recv, row_send, row_recv,
):
    rows, zs, qs, grps, real, width, tokens = shape
    n = zs * qs
    total = n * PAD
    row = lax.axis_index("row")
    me = lax.axis_index("lat") * grps + lax.axis_index("grp")
    z = me // qs
    q = lax.rem(me, qs)

    def at(shard):
        return {"lat": shard // grps, "grp": lax.rem(shard, grps)}

    def zpeer(d):
        return lax.rem(z + d, zs)

    def qpeer(d):
        return lax.rem(q + d, qs)

    def send(src, dst, s, r, dev):
        return pltpu.make_async_remote_copy(
            src_ref=src, dst_ref=dst, send_sem=s, recv_sem=r, device_id=dev, device_id_type=MESH
        )

    loads = [
        pltpu.make_async_copy(a, b, wsem.at[i])
        for i, (a, b) in enumerate(
            [
                (gate_hbm, wg), (up_hbm, wu), (down_hbm, wd), (enc_hbm, wenc), (dec_hbm, wdec),
                (pre_hbm, pre_ref), (post_hbm, post_ref), (encb_hbm, encb_ref),
                (decb_hbm, decb_ref), (stream_hbm, xs.at[me]),
            ]
        )
    ]
    for load in loads[5:] + loads[:5]:
        load.start()

    barrier = pltpu.get_barrier_semaphore()

    def hail(dev):
        pl.semaphore_signal(barrier, inc=1, device_id=dev, device_id_type=MESH)

    each(zs - 1, lambda i: hail(at(zpeer(i + 1) * qs + q)))
    each(qs - 1, lambda i: hail(at(z * qs + qpeer(i + 1))))
    each(rows - 1, lambda i: hail({"row": lax.rem(row + i + 1, rows)}))
    pl.semaphore_wait(barrier, zs - 1 + qs - 1 + rows - 1)

    def gather_copy(k, buf, shard, dev, slot):
        return send(buf.at[shard], buf.at[shard], ag_send.at[k, slot], ag_recv.at[k, shard], dev)

    def to_plane(k, buf, dz, shard, start):
        def one(i):
            c = gather_copy(k, buf, shard, at(z * qs + qpeer(i + 1)), dz * qs + i + 1)
            c.start() if start else c.wait_send()

        each(qs - 1, one)

    def gather_start(k, buf):
        each(
            zs - 1,
            lambda i: gather_copy(k, buf, me, at(zpeer(i + 1) * qs + q), (i + 1) * qs).start(),
        )
        to_plane(k, buf, 0, me, True)

    def gather_pass(k, buf):
        def one(i):
            shard = zpeer(i + 1) * qs + q
            gather_copy(k, buf, shard, at(shard), 0).wait_recv()
            to_plane(k, buf, i + 1, shard, True)

        each(zs - 1, one)

    def gather_end(k, buf, done):
        def one(dz):
            done(zpeer(dz) * qs + q)

            def two(i):
                shard = zpeer(dz) * qs + qpeer(i + 1)
                gather_copy(k, buf, shard, at(z * qs + qpeer(i + 1)), 0).wait_recv()
                done(shard)

            each(qs - 1, two)

        each(zs, one)

        def sent(dz):
            to_plane(k, buf, dz, zpeer(dz) * qs + q, False)

        each(zs, sent)
        each(
            zs - 1,
            lambda i: gather_copy(k, buf, me, at(zpeer(i + 1) * qs + q), (i + 1) * qs).wait_send(),
        )

    def plane_out(k, part, land, zz, dq):
        to = qpeer(dq)
        return send(
            part.at[zz * qs + to], land.at[q, zz],
            rs_send.at[k, zz * qs + dq], rs_recv.at[k, zz * qs + q], at(z * qs + to),
        )

    def plane_in(k, part, land, zz, dq):
        of = qpeer(dq)
        return send(
            part.at[zz * qs + of], land.at[of, zz],
            rs_send.at[k, zz * qs + dq], rs_recv.at[k, zz * qs + of], at(z * qs + of),
        )

    def line(k, mid, far, dz):
        to = zpeer(dz)
        return send(mid.at[to], far.at[z], rz_send.at[k, to], rz_recv.at[k, z], at(to * qs + q))

    def line_in(k, mid, far, dz):
        of = zpeer(dz)
        return send(mid.at[of], far.at[of], rz_send.at[k, of], rz_recv.at[k, of], at(of * qs + q))

    def scatter_start(k, part, land):
        def one(dz):
            zz = zpeer(dz + 1)
            each(qs - 1, lambda i: plane_out(k, part, land, zz, i + 1).start())

        each(zs, one)

    def scatter_sum(k, part, land, mid, far):
        def plane_sum(zz):
            each(qs - 1, lambda i: plane_in(k, part, land, zz, i + 1).wait_recv())
            acc = part[zz * qs + q].astype(f32)
            for i in range(1, qs):
                acc = acc + land[qpeer(i), zz].astype(f32)
            return acc

        def one(i):
            zz = zpeer(i + 1)
            mid[zz] = plane_sum(zz).astype(bf16)
            line(k, mid, far, i + 1).start()

        each(zs - 1, one)
        acc = plane_sum(z)
        for dz in range(1, zs):
            line_in(k, mid, far, dz).wait_recv()
            acc = acc + far[zpeer(dz)].astype(f32)
        return acc

    def scatter_end(k, part, land, mid, far):
        def one(dz):
            each(qs - 1, lambda i: plane_out(k, part, land, zpeer(dz), i + 1).wait_send())

        each(zs, one)
        each(zs - 1, lambda i: line(k, mid, far, i + 1).wait_send())

    def row_out(k, buf, d):
        return send(
            buf.at[row], buf.at[row], row_send.at[k, d], row_recv.at[k, row],
            {"row": lax.rem(row + d, rows)},
        )

    def row_start(k, buf):
        each(rows - 1, lambda i: row_out(k, buf, i + 1).start())

    def row_wait(k, buf):
        def one(i):
            of = lax.rem(row + i + 1, rows)
            send(
                buf.at[of], buf.at[of], row_send.at[k, 0], row_recv.at[k, of], {"row": of}
            ).wait_recv()
            row_out(k, buf, i + 1).wait_send()

        each(rows - 1, one)

    def row_sum(buf, *index):
        acc = buf[(0, *index)].astype(f32)
        for i in range(1, rows):
            acc = acc + buf[(i, *index)].astype(f32)
        return acc

    def block(i):
        return pl.ds(pl.multiple_of(i * PAD, PAD), PAD)

    def fill(v):
        return jnp.concatenate([v, jnp.zeros((PAD - real, v.shape[1]), v.dtype)], axis=0)

    def line_of(ref):
        return ref[...].reshape(1, ref.shape[0])

    def widen(buf, dst):
        def one(i):
            dst[block(i), :] = fill(buf[i].astype(f32)).astype(bf16)

        return one

    def cast(src, dst):
        tall = src.shape[0]
        chunk = 16

        def one(i):
            r = pl.ds(pl.multiple_of(i * chunk, chunk), chunk)
            dst[r, :] = src[r, :].astype(bf16)

        each(tall // chunk, one)

    loads[9].wait()
    gather_start(0, xs)
    for load in loads[5:9]:
        load.wait()
    gather_pass(0, xs)

    def norm_rows(i):
        x = fill(xs[i].astype(f32))
        xg[block(i), :] = (x * line_of(pre_ref)).astype(bf16)
        sbuf[row, block(i), :] = jnp.broadcast_to(
            jnp.sum(x * x, axis=1, keepdims=True), (PAD, 128)
        )

    gather_end(0, xs, norm_rows)
    row_start(0, sbuf)

    def project(buf, w):
        def one(c):
            buf[row, :, c] = jnp.dot(xg[...], w[:, c], preferred_element_type=f32).astype(bf16)

        column_tiles(w.shape[1], one)

    loads[0].wait()
    project(gbuf, wg)
    row_start(1, gbuf)
    loads[1].wait()
    project(ubuf, wu)
    row_start(2, ubuf)
    loads[3].wait()
    row_wait(0, sbuf)
    row_wait(1, gbuf)
    row_wait(2, ubuf)

    def activate(i):
        r = lax.rsqrt(row_sum(sbuf, block(i))[:, :1] / width + epsilon)
        g = row_sum(gbuf, block(i)) * r
        u = row_sum(ubuf, block(i)) * r
        hidden[block(i), :] = (jax.nn.gelu(g, approximate=True) * u).astype(bf16)

    each(n, activate)
    loads[2].wait()

    def down(c):
        v = jnp.dot(hidden[...], wd[:, c], preferred_element_type=f32)
        part1[:, :, c] = v.reshape(n, PAD, v.shape[1])[:, :real, :].astype(bf16)

    column_tiles(wd.shape[1], down)
    scatter_start(0, part1, land1)
    cast(wenc, enc16)
    output = scatter_sum(0, part1, land1, mid1, far1)
    tbuf[row] = jnp.broadcast_to(jnp.sum(output * output, axis=1, keepdims=True), (real, 128))
    row_start(3, tbuf)
    row_wait(3, tbuf)
    scale_out = lax.rsqrt(row_sum(tbuf)[:, :1] / width + epsilon)
    mine = xs[me].astype(f32) + output * scale_out * line_of(post_ref)
    stream_out = mine.astype(bf16)
    out_ref[...] = stream_out
    ys[me] = stream_out
    gather_start(1, ys)
    scatter_end(0, part1, land1, mid1, far1)
    loads[4].wait()
    gather_pass(1, ys)
    cast(wdec, dec16)
    gather_end(1, ys, widen(ys, inputs_ref))

    def encode(c):
        pbuf[row, :, c] = jnp.dot(
            inputs_ref[...], enc16[:, c], preferred_element_type=f32
        ).astype(bf16)

    column_tiles(enc16.shape[1], encode)
    row_start(4, pbuf)
    row_wait(4, pbuf)

    def softplus(i):
        p = sharpness * (row_sum(pbuf, block(i)) + line_of(encb_ref))
        e = jnp.exp(-jnp.abs(p))
        lat_ref[block(i), :] = (
            (jnp.maximum(p, 0.0) + jnp.log1p(e)) * (1.0 / sharpness)
        ).astype(bf16)
        preact[block(i), :] = jnp.where(p >= 0, 1.0, e) / (1.0 + e)

    each(n, softplus)

    def decode(c):
        v = jnp.dot(lat_ref[...], dec16[:, c], preferred_element_type=f32)
        part2[:, :, c] = v.reshape(n, PAD, v.shape[1])[:, :real, :].astype(bf16)

    column_tiles(dec16.shape[1], decode)
    scatter_start(1, part2, land2)
    recon = scatter_sum(1, part2, land2, mid2, far2)
    scale = 1.0 / math.sqrt(tokens)
    keep = lax.broadcasted_iota(jnp.int32, (PAD, 1), 0) < real
    resid = (recon + line_of(decb_ref) - ys[me].astype(f32)) * scale
    rs[me] = resid.astype(bf16)
    gather_start(2, rs)
    scatter_end(1, part2, land2, mid2, far2)
    gather_pass(2, rs)
    gather_end(2, rs, widen(rs, resid_ref))

    def back(c):
        bbuf[row, :, c] = lax.dot_general(
            resid_ref[...], dec16[c, :],
            (((1,), (1,)), ((), ())), preferred_element_type=f32,
        ).astype(bf16)

    column_tiles(dec16.shape[0], back)
    row_start(5, bbuf)

    gdecb_ref[...] = jnp.zeros_like(gdecb_ref)

    def dec_bias(i):
        gdecb_ref[...] += jnp.sum(rs[i].astype(f32), axis=0, keepdims=True)

    each(n, dec_bias)
    row_wait(5, bbuf)
    gencb_ref[...] = jnp.zeros_like(gencb_ref)

    def finish(i):
        g = (row_sum(bbuf, block(i)) + sparsity * scale) * preact[block(i), :]
        pgrad_ref[block(i), :] = g.astype(bf16)
        gencb_ref[...] += jnp.sum(jnp.where(keep, g, 0.0), axis=0, keepdims=True)

    each(n, finish)


def body(
    split, sizes,
    stream_in, pre_gain, gate_weight, up_weight, down_weight, post_gain,
    enc_weight, enc_bias, dec_weight, dec_bias,
):
    rows, zs, qs, grps = sizes
    n = zs * qs
    real, d = stream_in.shape
    hid = gate_weight.shape[1]
    lat = enc_weight.shape[1]
    total = n * PAD
    shape = (rows, zs, qs, grps, real, d * rows, real * n)
    vmem = pltpu.VMEM
    scratch = [
        vmem((d, hid), bf16), vmem((d, hid), bf16), vmem((hid, d), bf16),
        vmem((d, lat), f32), vmem((lat, d), f32), vmem((d, lat), bf16), vmem((lat, d), bf16),
        vmem((n, real, d), bf16), vmem((total, d), bf16),
        vmem((rows, total, hid), bf16), vmem((rows, total, hid), bf16),
        vmem((rows, total, 128), f32), vmem((total, hid), bf16), vmem((8, 128), f32),
        vmem((n, real, d), bf16), vmem((qs, zs, real, d), bf16),
        vmem((zs, real, d), bf16), vmem((zs, real, d), bf16),
        vmem((rows, real, 128), f32), vmem((n, real, d), bf16),
        vmem((rows, total, lat), bf16), vmem((total, lat), f32),
        vmem((n, real, d), bf16), vmem((qs, zs, real, d), bf16),
        vmem((zs, real, d), bf16), vmem((zs, real, d), bf16),
        vmem((n, real, d), bf16), vmem((rows, total, lat), bf16),
        vmem((d,), f32), vmem((d,), f32), vmem((lat,), f32), vmem((d,), f32),
        pltpu.SemaphoreType.DMA((10,)),
        pltpu.SemaphoreType.DMA((3, n)), pltpu.SemaphoreType.DMA((3, n)),
        pltpu.SemaphoreType.DMA((2, n)), pltpu.SemaphoreType.DMA((2, n)),
        pltpu.SemaphoreType.DMA((2, zs)), pltpu.SemaphoreType.DMA((2, zs)),
        pltpu.SemaphoreType.DMA((6, rows)), pltpu.SemaphoreType.DMA((6, rows)),
    ]
    here = pl.BlockSpec(memory_space=pltpu.VMEM)
    there = pl.BlockSpec(memory_space=pl.ANY)
    sds = jax.ShapeDtypeStruct
    out, inputs, latents, resid, pgrad, gencb, gdecb = pl.pallas_call(
        functools.partial(kernel, shape),
        out_shape=(
            sds((real, d), bf16), sds((total, d), bf16), sds((total, lat), bf16),
            sds((total, d), bf16), sds((total, lat), bf16), sds((1, lat), f32), sds((1, d), f32),
        ),
        in_specs=[there] * 10,
        out_specs=[here] * 7,
        scratch_shapes=scratch,
        compiler_params=pltpu.CompilerParams(
            collective_id=0, has_side_effects=True, vmem_limit_bytes=60 * 1024 * 1024
        ),
    )(
        stream_in, pre_gain, post_gain, enc_bias, dec_bias,
        gate_weight, up_weight, down_weight, enc_weight, dec_weight,
    )
    grad_dec = jnp.dot(latents.T, resid, preferred_element_type=f32)
    grad_enc = jnp.dot(inputs.T, pgrad, preferred_element_type=f32)
    return (out, grad_enc, gencb[0], grad_dec, gdecb[0])


def solution(mesh):
    rows, lats, grps = (mesh.shape[a] for a in ("row", "lat", "grp"))
    inner = max(i for i in range(1, lats + 1) if lats % i == 0 and i * i <= lats)
    sizes = (rows, lats // inner, inner * grps, grps)
    both = ("lat", "grp")
    placed = (
        P(both, "row"), P("row"), P("row", both), P("row", both), P(both, "row"),
        P("row"), P("row", both), P(both), P(both, "row"), P("row"),
    )
    return jax.shard_map(
        functools.partial(body, None, sizes),
        mesh=mesh,
        in_specs=placed,
        out_specs=(P(both, "row"), P("row", both), P(both), P(both, "row"), P("row")),
        check_vma=False,
    )
```

```python
import functools
import math

import jax
import jax.numpy as jnp
from jax import lax
from jax.experimental import pallas as pl
from jax.experimental.pallas import tpu as pltpu
from jax.sharding import PartitionSpec as P

epsilon = 1e-06
sparsity = 0.2
sharpness = 4.0
PAD = 16
f32 = jnp.float32
bf16 = jnp.bfloat16
MESH = pl.DeviceIdType.MESH


def each(n, f):
    if n > 0:
        lax.fori_loop(0, n, lambda i, c: (f(i), c)[1], 0)


def column_tiles(width, f, tile=256):
    whole = width // tile
    each(whole, lambda i: f(pl.ds(pl.multiple_of(i * tile, tile), tile)))
    if width % tile:
        f(pl.ds(whole * tile, width % tile))


def kernel(
    shape,
    stream_hbm, pre_hbm, post_hbm, encb_hbm, decb_hbm,
    gate_hbm, up_hbm, down_hbm, enc_hbm, dec_hbm,
    out_ref, inputs_ref, lat_ref, resid_ref, pgrad_ref, gencb_ref, gdecb_ref,
    wg, wu, wd, wenc, wdec, enc16, dec16,
    xs, xg, gbuf, ubuf, sbuf, hidden, squares,
    part1, land1, mid1, far1, tbuf, ys,
    pbuf, preact, part2, land2, mid2, far2, rs, bbuf,
    pre_ref, post_ref, encb_ref, decb_ref,
    wsem,
    ag_send, ag_recv, rs_send, rs_recv, rz_send, rz_recv, row_send, row_recv,
):
    rows, zs, qs, grps, real, width, tokens = shape
    n = zs * qs
    total = n * PAD
    row = lax.axis_index("row")
    me = lax.axis_index("lat") * grps + lax.axis_index("grp")
    z = me // qs
    q = lax.rem(me, qs)

    def at(shard):
        return {"lat": shard // grps, "grp": lax.rem(shard, grps)}

    def zpeer(d):
        return lax.rem(z + d, zs)

    def qpeer(d):
        return lax.rem(q + d, qs)

    def send(src, dst, s, r, dev):
        return pltpu.make_async_remote_copy(
            src_ref=src, dst_ref=dst, send_sem=s, recv_sem=r, device_id=dev, device_id_type=MESH
        )

    loads = [
        pltpu.make_async_copy(a, b, wsem.at[i])
        for i, (a, b) in enumerate(
            [
                (gate_hbm, wg), (up_hbm, wu), (down_hbm, wd), (enc_hbm, wenc), (dec_hbm, wdec),
                (pre_hbm, pre_ref), (post_hbm, post_ref), (encb_hbm, encb_ref),
                (decb_hbm, decb_ref), (stream_hbm, xs.at[me]),
            ]
        )
    ]
    for load in loads[5:] + loads[:5]:
        load.start()

    barrier = pltpu.get_barrier_semaphore()

    def hail(dev):
        pl.semaphore_signal(barrier, inc=1, device_id=dev, device_id_type=MESH)

    each(zs - 1, lambda i: hail(at(zpeer(i + 1) * qs + q)))
    each(qs - 1, lambda i: hail(at(z * qs + qpeer(i + 1))))
    each(rows - 1, lambda i: hail({"row": lax.rem(row + i + 1, rows)}))
    pl.semaphore_wait(barrier, zs - 1 + qs - 1 + rows - 1)

    def gather_copy(k, buf, shard, dev, slot):
        return send(buf.at[shard], buf.at[shard], ag_send.at[k, slot], ag_recv.at[k, shard], dev)

    def to_plane(k, buf, dz, shard, start):
        def one(i):
            c = gather_copy(k, buf, shard, at(z * qs + qpeer(i + 1)), dz * qs + i + 1)
            c.start() if start else c.wait_send()

        each(qs - 1, one)

    def gather_start(k, buf):
        each(
            zs - 1,
            lambda i: gather_copy(k, buf, me, at(zpeer(i + 1) * qs + q), (i + 1) * qs).start(),
        )
        to_plane(k, buf, 0, me, True)

    def gather_pass(k, buf):
        def one(i):
            shard = zpeer(i + 1) * qs + q
            gather_copy(k, buf, shard, at(shard), 0).wait_recv()
            to_plane(k, buf, i + 1, shard, True)

        each(zs - 1, one)

    def gather_end(k, buf, done):
        def one(dz):
            done(zpeer(dz) * qs + q)

            def two(i):
                shard = zpeer(dz) * qs + qpeer(i + 1)
                gather_copy(k, buf, shard, at(z * qs + qpeer(i + 1)), 0).wait_recv()
                done(shard)

            each(qs - 1, two)

        each(zs, one)

        def sent(dz):
            to_plane(k, buf, dz, zpeer(dz) * qs + q, False)

        each(zs, sent)
        each(
            zs - 1,
            lambda i: gather_copy(k, buf, me, at(zpeer(i + 1) * qs + q), (i + 1) * qs).wait_send(),
        )

    def plane_out(k, part, land, zz, dq):
        to = qpeer(dq)
        return send(
            part.at[zz * qs + to], land.at[q, zz],
            rs_send.at[k, zz * qs + dq], rs_recv.at[k, zz * qs + q], at(z * qs + to),
        )

    def plane_in(k, part, land, zz, dq):
        of = qpeer(dq)
        return send(
            part.at[zz * qs + of], land.at[of, zz],
            rs_send.at[k, zz * qs + dq], rs_recv.at[k, zz * qs + of], at(z * qs + of),
        )

    def line(k, mid, far, dz):
        to = zpeer(dz)
        return send(mid.at[to], far.at[z], rz_send.at[k, to], rz_recv.at[k, z], at(to * qs + q))

    def line_in(k, mid, far, dz):
        of = zpeer(dz)
        return send(mid.at[of], far.at[of], rz_send.at[k, of], rz_recv.at[k, of], at(of * qs + q))

    def scatter_start(k, part, land):
        def one(dz):
            zz = zpeer(dz + 1)
            each(qs - 1, lambda i: plane_out(k, part, land, zz, i + 1).start())

        each(zs, one)

    def scatter_sum(k, part, land, mid, far):
        def plane_sum(zz):
            each(qs - 1, lambda i: plane_in(k, part, land, zz, i + 1).wait_recv())
            acc = part[zz * qs + q].astype(f32)
            for i in range(1, qs):
                acc = acc + land[qpeer(i), zz].astype(f32)
            return acc

        def one(i):
            zz = zpeer(i + 1)
            mid[zz] = plane_sum(zz).astype(bf16)
            line(k, mid, far, i + 1).start()

        each(zs - 1, one)
        acc = plane_sum(z)
        for dz in range(1, zs):
            line_in(k, mid, far, dz).wait_recv()
            acc = acc + far[zpeer(dz)].astype(f32)
        return acc

    def scatter_end(k, part, land, mid, far):
        def one(dz):
            each(qs - 1, lambda i: plane_out(k, part, land, zpeer(dz), i + 1).wait_send())

        each(zs, one)
        each(zs - 1, lambda i: line(k, mid, far, i + 1).wait_send())

    def row_out(k, buf, d):
        return send(
            buf.at[row], buf.at[row], row_send.at[k, d], row_recv.at[k, row],
            {"row": lax.rem(row + d, rows)},
        )

    def row_start(k, buf):
        each(rows - 1, lambda i: row_out(k, buf, i + 1).start())

    def row_piece(k, buf, c):
        def one(i):
            send(
                buf.at[row, :, c], buf.at[row, :, c], row_send.at[k, i + 1],
                row_recv.at[k, row], {"row": lax.rem(row + i + 1, rows)},
            ).start()

        each(rows - 1, one)

    def row_wait(k, buf):
        def one(i):
            of = lax.rem(row + i + 1, rows)
            send(
                buf.at[of], buf.at[of], row_send.at[k, 0], row_recv.at[k, of], {"row": of}
            ).wait_recv()
            row_out(k, buf, i + 1).wait_send()

        each(rows - 1, one)

    def row_sum(buf, *index):
        acc = buf[(0, *index)].astype(f32)
        for i in range(1, rows):
            acc = acc + buf[(i, *index)].astype(f32)
        return acc

    def block(i):
        return pl.ds(pl.multiple_of(i * PAD, PAD), PAD)

    def fill(v):
        return jnp.concatenate([v, jnp.zeros((PAD - real, v.shape[1]), v.dtype)], axis=0)

    def line_of(ref):
        return ref[...].reshape(1, ref.shape[0])

    def widen(buf, dst):
        def one(i):
            dst[block(i), :] = fill(buf[i].astype(f32)).astype(bf16)

        return one

    def cast(src, dst):
        tall = src.shape[0]
        chunk = 16

        def one(i):
            r = pl.ds(pl.multiple_of(i * chunk, chunk), chunk)
            dst[r, :] = src[r, :].astype(bf16)

        each(tall // chunk, one)

    loads[9].wait()
    gather_start(0, xs)
    for load in loads[5:9]:
        load.wait()
    gather_pass(0, xs)

    def norm_rows(i):
        x = fill(xs[i].astype(f32))
        xg[block(i), :] = (x * line_of(pre_ref)).astype(bf16)
        sbuf[row, block(i), :] = jnp.broadcast_to(
            jnp.sum(x * x, axis=1, keepdims=True), (PAD, 128)
        )

    gather_end(0, xs, norm_rows)
    row_start(0, sbuf)

    def project(k, buf, w):
        def one(c):
            buf[row, :, c] = jnp.dot(xg[...], w[:, c], preferred_element_type=f32).astype(bf16)
            row_piece(k, buf, c)

        column_tiles(w.shape[1], one)

    loads[0].wait()
    project(1, gbuf, wg)
    loads[1].wait()
    project(2, ubuf, wu)
    loads[3].wait()
    row_wait(0, sbuf)
    row_wait(1, gbuf)
    row_wait(2, ubuf)

    def activate(i):
        r = lax.rsqrt(row_sum(sbuf, block(i))[:, :1] / width + epsilon)
        g = row_sum(gbuf, block(i)) * r
        u = row_sum(ubuf, block(i)) * r
        hidden[block(i), :] = (jax.nn.gelu(g, approximate=True) * u).astype(bf16)

    each(n, activate)
    loads[2].wait()

    def down(c):
        v = jnp.dot(hidden[...], wd[:, c], preferred_element_type=f32)
        part1[:, :, c] = v.reshape(n, PAD, v.shape[1])[:, :real, :].astype(bf16)

    column_tiles(wd.shape[1], down)
    scatter_start(0, part1, land1)
    cast(wenc, enc16)
    output = scatter_sum(0, part1, land1, mid1, far1)
    tbuf[row] = jnp.broadcast_to(jnp.sum(output * output, axis=1, keepdims=True), (real, 128))
    row_start(3, tbuf)
    row_wait(3, tbuf)
    scale_out = lax.rsqrt(row_sum(tbuf)[:, :1] / width + epsilon)
    mine = xs[me].astype(f32) + output * scale_out * line_of(post_ref)
    stream_out = mine.astype(bf16)
    out_ref[...] = stream_out
    ys[me] = stream_out
    gather_start(1, ys)
    scatter_end(0, part1, land1, mid1, far1)
    loads[4].wait()
    gather_pass(1, ys)
    cast(wdec, dec16)
    gather_end(1, ys, widen(ys, inputs_ref))

    def encode(c):
        pbuf[row, :, c] = jnp.dot(
            inputs_ref[...], enc16[:, c], preferred_element_type=f32
        ).astype(bf16)
        row_piece(4, pbuf, c)

    column_tiles(enc16.shape[1], encode)
    row_wait(4, pbuf)

    def softplus(i):
        p = sharpness * (row_sum(pbuf, block(i)) + line_of(encb_ref))
        e = jnp.exp(-jnp.abs(p))
        lat_ref[block(i), :] = (
            (jnp.maximum(p, 0.0) + jnp.log1p(e)) * (1.0 / sharpness)
        ).astype(bf16)
        preact[block(i), :] = jnp.where(p >= 0, 1.0, e) / (1.0 + e)

    each(n, softplus)

    def decode(c):
        v = jnp.dot(lat_ref[...], dec16[:, c], preferred_element_type=f32)
        part2[:, :, c] = v.reshape(n, PAD, v.shape[1])[:, :real, :].astype(bf16)

    column_tiles(dec16.shape[1], decode)
    scatter_start(1, part2, land2)
    recon = scatter_sum(1, part2, land2, mid2, far2)
    scale = 1.0 / math.sqrt(tokens)
    keep = lax.broadcasted_iota(jnp.int32, (PAD, 1), 0) < real
    resid = (recon + line_of(decb_ref) - ys[me].astype(f32)) * scale
    rs[me] = resid.astype(bf16)
    gather_start(2, rs)
    scatter_end(1, part2, land2, mid2, far2)
    gather_pass(2, rs)
    gather_end(2, rs, widen(rs, resid_ref))

    def back(c):
        bbuf[row, :, c] = lax.dot_general(
            resid_ref[...], dec16[c, :],
            (((1,), (1,)), ((), ())), preferred_element_type=f32,
        ).astype(bf16)
        row_piece(5, bbuf, c)

    column_tiles(dec16.shape[0], back)

    gdecb_ref[...] = jnp.zeros_like(gdecb_ref)

    def dec_bias(i):
        gdecb_ref[...] += jnp.sum(rs[i].astype(f32), axis=0, keepdims=True)

    each(n, dec_bias)
    row_wait(5, bbuf)
    gencb_ref[...] = jnp.zeros_like(gencb_ref)

    def finish(i):
        g = (row_sum(bbuf, block(i)) + sparsity * scale) * preact[block(i), :]
        pgrad_ref[block(i), :] = g.astype(bf16)
        gencb_ref[...] += jnp.sum(jnp.where(keep, g, 0.0), axis=0, keepdims=True)

    each(n, finish)


def gradients(
    steps, inputs_ref, pgrad_ref, lat_ref, resid_ref, gencb_in, gdecb_in, out_in,
    genc_ref, gdec_ref, gencb_ref, gdecb_ref, out_ref,
):
    i = pl.program_id(0)
    over_rows = (((0,), (0,)), ((), ()))

    @pl.when(i == 0)
    def _():
        gencb_ref[...] = gencb_in[...].reshape(gencb_ref.shape)
        gdecb_ref[...] = gdecb_in[...].reshape(gdecb_ref.shape)
        out_ref[...] = out_in[...]

    @pl.when(i < steps)
    def _():
        genc_ref[...] = lax.dot_general(
            inputs_ref[...], pgrad_ref[...], over_rows, preferred_element_type=f32
        )

    @pl.when(i >= steps)
    def _():
        gdec_ref[...] = lax.dot_general(
            lat_ref[...], resid_ref[...], over_rows, preferred_element_type=f32
        )


def body(
    split, sizes,
    stream_in, pre_gain, gate_weight, up_weight, down_weight, post_gain,
    enc_weight, enc_bias, dec_weight, dec_bias,
):
    rows, zs, qs, grps = sizes
    n = zs * qs
    real, d = stream_in.shape
    hid = gate_weight.shape[1]
    lat = enc_weight.shape[1]
    total = n * PAD
    shape = (rows, zs, qs, grps, real, d * rows, real * n)
    vmem = pltpu.VMEM
    scratch = [
        vmem((d, hid), bf16), vmem((d, hid), bf16), vmem((hid, d), bf16),
        vmem((d, lat), f32), vmem((lat, d), f32), vmem((d, lat), bf16), vmem((lat, d), bf16),
        vmem((n, real, d), bf16), vmem((total, d), bf16),
        vmem((rows, total, hid), bf16), vmem((rows, total, hid), bf16),
        vmem((rows, total, 128), f32), vmem((total, hid), bf16), vmem((8, 128), f32),
        vmem((n, real, d), bf16), vmem((qs, zs, real, d), bf16),
        vmem((zs, real, d), bf16), vmem((zs, real, d), bf16),
        vmem((rows, real, 128), f32), vmem((n, real, d), bf16),
        vmem((rows, total, lat), bf16), vmem((total, lat), f32),
        vmem((n, real, d), bf16), vmem((qs, zs, real, d), bf16),
        vmem((zs, real, d), bf16), vmem((zs, real, d), bf16),
        vmem((n, real, d), bf16), vmem((rows, total, lat), bf16),
        vmem((d,), f32), vmem((d,), f32), vmem((lat,), f32), vmem((d,), f32),
        pltpu.SemaphoreType.DMA((10,)),
        pltpu.SemaphoreType.DMA((3, n)), pltpu.SemaphoreType.DMA((3, n)),
        pltpu.SemaphoreType.DMA((2, n)), pltpu.SemaphoreType.DMA((2, n)),
        pltpu.SemaphoreType.DMA((2, zs)), pltpu.SemaphoreType.DMA((2, zs)),
        pltpu.SemaphoreType.DMA((6, rows)), pltpu.SemaphoreType.DMA((6, rows)),
    ]
    here = pl.BlockSpec(memory_space=pltpu.VMEM)
    there = pl.BlockSpec(memory_space=pl.ANY)
    sds = jax.ShapeDtypeStruct
    out, inputs, latents, resid, pgrad, gencb, gdecb = pl.pallas_call(
        functools.partial(kernel, shape),
        out_shape=(
            sds((real, d), bf16), sds((total, d), bf16), sds((total, lat), bf16),
            sds((total, d), bf16), sds((total, lat), bf16), sds((1, lat), f32), sds((1, d), f32),
        ),
        in_specs=[there] * 10,
        out_specs=[here] * 7,
        scratch_shapes=scratch,
        compiler_params=pltpu.CompilerParams(
            collective_id=0, has_side_effects=True, vmem_limit_bytes=60 * 1024 * 1024
        ),
    )(
        stream_in, pre_gain, post_gain, enc_bias, dec_bias,
        gate_weight, up_weight, down_weight, enc_weight, dec_weight,
    )
    tall_enc = 256 if d % 256 == 0 else d
    tall_dec = 256 if lat % 256 == 0 else lat
    steps = d // tall_enc

    def whole(*dims):
        return pl.BlockSpec(dims, lambda i: (0,) * len(dims))

    grad_enc, grad_dec, grad_encb, grad_decb, stream_out = pl.pallas_call(
        functools.partial(gradients, steps),
        grid=(steps + lat // tall_dec,),
        out_shape=(
            sds((d, lat), f32), sds((lat, d), f32), sds((lat,), f32), sds((d,), f32),
            sds((real, d), bf16),
        ),
        in_specs=[
            pl.BlockSpec((total, tall_enc), lambda i: (0, jnp.minimum(i, steps - 1))),
            whole(total, lat),
            pl.BlockSpec((total, tall_dec), lambda i: (0, jnp.maximum(i - steps, 0))),
            whole(total, d), whole(1, lat), whole(1, d), whole(real, d),
        ],
        out_specs=(
            pl.BlockSpec((tall_enc, lat), lambda i: (jnp.minimum(i, steps - 1), 0)),
            pl.BlockSpec((tall_dec, d), lambda i: (jnp.maximum(i - steps, 0), 0)),
            whole(lat), whole(d), whole(real, d),
        ),
        compiler_params=pltpu.CompilerParams(vmem_limit_bytes=32 * 1024 * 1024),
    )(inputs, pgrad, latents, resid, gencb, gdecb, out)
    return (stream_out, grad_enc, grad_encb, grad_dec, grad_decb)


def solution(mesh):
    rows, lats, grps = (mesh.shape[a] for a in ("row", "lat", "grp"))
    inner = max(i for i in range(1, lats + 1) if lats % i == 0 and i * i <= lats)
    sizes = (rows, lats // inner, inner * grps, grps)
    both = ("lat", "grp")
    placed = (
        P(both, "row"), P("row"), P("row", both), P("row", both), P(both, "row"),
        P("row"), P("row", both), P(both), P(both, "row"), P("row"),
    )
    return jax.shard_map(
        functools.partial(body, None, sizes),
        mesh=mesh,
        in_specs=placed,
        out_specs=(P(both, "row"), P("row", both), P(both), P(both, "row"), P("row")),
        check_vma=False,
    )
```
